32 devices in a mesh: section: 4 (over z), dom: 8 (over y, x, core).
Axes of the slice: x: 2, y: 2, z: 4, core: 2. Of those that a mesh axis runs over, the one named last changes fastest.
Arguments:
- images: bfloat16 [4, 32, 65536], P('section', None, 'dom'), may hold values from -48 to 48
- weights: bfloat16 [8, 1024, 64, 256], P('section', 'dom'), may hold values from -0.625 to 0.625
- bias: bfloat16 [8, 65536], P('section', 'dom'), may hold values from -12 to 12
- pattern: int32 [8, 1024, 4], P('section'), may hold values from 0 to 1023, as said below
- counts: int32 [8, 1024], P('section', 'dom'), may hold values from 2 to 4, as said below
Outputs:
- scores: bfloat16 [4, 32, 65536], P('section', None, 'dom')
The draws below stay inside these ranges and needn't reach their ends.
Inputs may be any that keep to these rules, and one draw needn't show every extreme that they name: `pattern`: A partition is the 128 consecutive column blocks of one neuron partition (and the row blocks of the same numbers). In each layer, slot 0 of every column block names a row block of its own partition; all slots of one partition's column blocks that name a row block of another partition name the same block of that partition, and every other partition is named so by slot 1 of some column block. Only the first counts[l, n] slots of a column block are live. In each layer every partition has a column block with all 4 slots live.
All inputs are finite; a program needn't handle non-finite values.
Results may differ from the reference program's by a relative error of at most 0.02.
Values may be sent and summed in bfloat16 or wider, within the bound.
A program may use at most 128 MiB of HBM per device.

```python
import jax
import jax.numpy as jnp
from jax import lax

N = 65536
BS = 64
K = 4
IMAGES = 32
NB = 1024
BLOCKS_DEV = 128
LAYERS = 8
MICRO = 4


def draw_pattern(key, part):
    part_count = NB // BLOCKS_DEV
    base = jax.random.fold_in(key, 11)
    key_pick, key_cand, key_turn = jax.random.split(base, 3)
    picked_block = jax.random.randint(key_pick, (LAYERS, part_count, part_count), 0, BLOCKS_DEV)
    candidate = jax.random.randint(key_cand, (LAYERS, part_count, BLOCKS_DEV, K), 0, BLOCKS_DEV + part_count - 1)
    turn = jax.random.randint(key_turn, (LAYERS, part_count, 1, 1), 0, part_count - 1)
    part_ids = jnp.arange(part_count).reshape(1, part_count, 1, 1)
    column_ids = jnp.arange(BLOCKS_DEV).reshape(1, 1, BLOCKS_DEV, 1)
    slot_ids = jnp.arange(K).reshape(1, 1, 1, K)
    is_local = (candidate < BLOCKS_DEV) | (slot_ids == 0)
    offset = candidate - BLOCKS_DEV + 1
    slot_one = (slot_ids == 1) & (column_ids < part_count - 1)
    offset = jnp.where(slot_one, 1 + (column_ids + turn) % (part_count - 1), offset)
    is_local = jnp.where(slot_one, False, is_local)
    offset = jnp.where(is_local, 1, offset)
    peers = (part_ids + offset) % part_count
    peers = jnp.broadcast_to(peers, (LAYERS, part_count, BLOCKS_DEV, K))
    chosen = jnp.take_along_axis(picked_block, peers.reshape(LAYERS, part_count, BLOCKS_DEV * K), axis=2)
    remote = peers * BLOCKS_DEV + chosen.reshape(LAYERS, part_count, BLOCKS_DEV, K)
    local_rows = part_ids * BLOCKS_DEV + candidate % BLOCKS_DEV
    result = jnp.where(is_local, local_rows, remote)
    return result.reshape(LAYERS, NB, K).astype(jnp.int32)


def draw_counts(key, part):
    part_count = NB // BLOCKS_DEV
    base = jax.random.fold_in(key, 23)
    key_count, key_full = jax.random.split(base, 2)
    drawn = jax.random.randint(key_count, (LAYERS, NB), 2, K + 1)
    chosen = jax.random.randint(key_full, (LAYERS, part_count), 0, BLOCKS_DEV)
    column_ids = jnp.arange(NB) % BLOCKS_DEV
    part_ids = jnp.arange(NB) // BLOCKS_DEV
    full_column = column_ids[None, :] == jnp.take(chosen, part_ids, axis=1)
    return jnp.where(full_column, K, drawn).astype(jnp.int32)


def steps_of(stream_key, dims, cuts, smallest, largest):
    gain = 1.0
    for axis_at, blocks in cuts:
        heights = jax.random.uniform(jax.random.fold_in(jax.random.fold_in(stream_key, 6), axis_at), (blocks,), jnp.float32, smallest / len(cuts), largest / len(cuts))
        gain = gain * jnp.repeat(jnp.exp(heights), dims[axis_at] // blocks).reshape((-1,) + (1,) * (len(dims) - 1 - axis_at))
    return gain


def gaussian(key, dims, deviation, reach, cuts=(), dtype=jnp.bfloat16):
    values = deviation * jax.random.normal(key, dims, jnp.float32)
    if cuts:
        values = values * steps_of(key, dims, cuts, -0.22, 0.18)
    return jnp.clip(values, -reach, reach).astype(dtype)


def setup_inputs(seed: int = 0) -> dict:
    splits = jax.random.split(jax.random.key(seed), 6)
    images = gaussian(splits[0], (MICRO, IMAGES, N), 8.0, 48.0, ((0, 4), (2, 8)))
    weights = gaussian(splits[1], (LAYERS, NB, BS, K * BS), (BS * (K + 2) // 4) ** -0.5, 0.625, ((0, 4), (1, 8)))
    bias = gaussian(splits[2], (LAYERS, N), 2.0, 12.0, ((0, 4), (1, 8)))
    pattern = draw_pattern(jax.random.fold_in(splits[5], 71), 0)
    counts = draw_counts(jax.random.fold_in(splits[5], 71), 0)
    return dict(images=images, weights=weights, bias=bias, pattern=pattern, counts=counts)


def reference(images, weights, bias, pattern, counts):
    live_slots = (jnp.arange(K)[None, None, :] < counts[:, :, None]).astype(jnp.float32)

    def run_micro(current):
        image_rows = current.shape[0]

        def layer_step(current, pieces):
            weight_block, bias_row, block_rows, live_row = pieces
            blocks = current.reshape(image_rows, NB, BS).astype(jnp.float32)
            gathered = jnp.take(blocks, block_rows.reshape(-1).astype(jnp.int32), axis=1)
            gathered = gathered.reshape(image_rows, NB, K, BS)
            weight_full = weight_block.astype(jnp.float32).reshape(NB, BS, K, BS) * live_row[:, None, :, None]
            pre_act = jnp.einsum("bnks,noks->bno", gathered, weight_full).reshape(image_rows, NB * BS)
            pre_act = pre_act + bias_row.astype(jnp.float32)[None, :]
            return jnp.clip(pre_act, 0.0, 32.0).astype(jnp.bfloat16), None

        result, _ = lax.scan(layer_step, current, (weights, bias, pattern, live_slots))
        return result

    return lax.map(run_micro, images)
```

```python
import functools

import jax
import jax.numpy as jnp
from jax import lax
from jax.experimental import pallas as pl
from jax.experimental.pallas import tpu as pltpu
from jax.sharding import PartitionSpec as P

MESH = pl.DeviceIdType.MESH
CHUNKS = 4


def prepare_tables(pattern, counts, per_part, part_count, my_part):
    layer_count = pattern.shape[0]
    slot_count = pattern.shape[2]
    block_table = pattern.reshape(layer_count, part_count, per_part * slot_count)
    owners = block_table // per_part
    wanted = jnp.max(jnp.where(owners == my_part, block_table % per_part, 0), axis=2)
    own_rows = lax.dynamic_slice_in_dim(pattern, my_part * per_part, per_part, 1)
    own_owners = own_rows // per_part
    slots = jnp.arange(slot_count, dtype=jnp.int32)[None, None, :]
    local = (own_rows % per_part) ^ (slots & 1)
    remote = per_part + (my_part - own_owners + part_count) % part_count - 1
    source = jnp.where(own_owners == my_part, local, remote)
    source = jnp.where(slots < counts[:, :, None], source, per_part + part_count - 1)
    return wanted, source.reshape(layer_count, per_part * slot_count)


def kernel(
    section_count, part_count, wanted_ref, source_ref, images_ref, weights_ref, bias_ref, out_ref,
    held, inbox, outbox, table, going, coming,
    weight_sem, own_sem, feed_sem, in_sem, out_sem, result_sem, going_sem, coming_sem,
):
    my_section = lax.axis_index("section")
    me = lax.axis_index("dom")
    layer_count, quads = weights_ref.shape[0], weights_ref.shape[1]
    micro_count, tiles, rows, lanes = inbox.shape
    per_chunk = tiles // CHUNKS
    last = section_count - 1
    others = part_count - 1

    loads = [
        pltpu.make_async_copy(weights_ref.at[l], held.at[l], weight_sem.at[l])
        for l in range(layer_count)
    ]
    for load in loads:
        load.start()

    barrier = pltpu.get_barrier_semaphore()

    def greet_part(step, carry):
        pl.semaphore_signal(
            barrier, inc=1, device_id=(my_section, lax.rem(me + step, part_count)), device_id_type=MESH
        )
        return carry

    def greet_section(step, carry):
        pl.semaphore_signal(
            barrier, inc=1, device_id=(lax.rem(my_section + step, section_count), me), device_id_type=MESH
        )
        return carry

    lax.fori_loop(1, part_count, greet_part, 0)
    lax.fori_loop(1, section_count, greet_section, 0)
    pl.semaphore_wait(barrier, others + section_count - 1)

    def chunk_of(c):
        return pl.ds(c * per_chunk, per_chunk)

    def feed(c):
        return pltpu.make_async_remote_copy(
            src_ref=images_ref.at[chunk_of(c)], dst_ref=inbox.at[my_section, chunk_of(c)],
            send_sem=feed_sem.at[c], recv_sem=in_sem.at[my_section, c],
            device_id=(0, me), device_id_type=MESH,
        )

    def forward(m, c):
        return pltpu.make_async_remote_copy(
            src_ref=outbox.at[m, chunk_of(c)], dst_ref=inbox.at[m, chunk_of(c)],
            send_sem=out_sem.at[m, c], recv_sem=in_sem.at[m, c],
            device_id=(lax.rem(my_section + 1, section_count), me), device_id_type=MESH,
        )

    def deliver(m, c):
        return pltpu.make_async_remote_copy(
            src_ref=outbox.at[m, chunk_of(c)], dst_ref=out_ref.at[chunk_of(c)],
            send_sem=out_sem.at[m, c], recv_sem=result_sem.at[c],
            device_id=(m, me), device_id_type=MESH,
        )

    @pl.when(my_section != 0)
    def _():
        for c in range(CHUNKS):
            feed(c).start()

    low = lax.broadcasted_iota(jnp.int32, (rows, lanes), 1) < lanes // 2
    table[0, 2 * tiles + others] = jnp.zeros((rows, lanes), jnp.bfloat16)
    table[1, 2 * tiles + others] = jnp.zeros((rows, lanes), jnp.bfloat16)

    def turned(x):
        return pltpu.roll(x.astype(jnp.float32), lanes // 2, 1).astype(jnp.bfloat16)

    def stage(m, carry):
        @pl.when((my_section != 0) | (m != 0))
        def _():
            for c in range(CHUNKS):
                forward(m, c).wait_recv()

        @pl.when((my_section == 0) & (m == 0))
        def _():
            own = pltpu.make_async_copy(images_ref, inbox.at[0], own_sem)
            own.start()
            own.wait()
            for load in loads:
                load.wait()

        @pl.when((my_section != 0) & (m == 0))
        def _():
            for load in loads:
                load.wait()

        def enter(q, carry):
            x = inbox[m, q]
            table[0, 2 * q] = x
            table[0, 2 * q + 1] = turned(x)
            return carry

        lax.fori_loop(0, tiles, enter, 0, unroll=4)

        for l in range(layer_count):
            now, later = l % 2, (l + 1) % 2

            def send(step, carry, l=l, now=now):
                peer = lax.rem(me + step, part_count)
                block = wanted_ref[l, peer]
                going[m, l, step - 1] = jnp.where(low, table[now, block], table[now, block ^ 1])
                pltpu.make_async_remote_copy(
                    src_ref=going.at[m, l, step - 1], dst_ref=coming.at[m, l, step - 1],
                    send_sem=going_sem.at[m, l], recv_sem=coming_sem.at[m, l],
                    device_id=(my_section, peer), device_id_type=MESH,
                ).start()
                return carry

            lax.fori_loop(1, part_count, send, 0)
            pltpu.make_async_remote_copy(
                src_ref=going.at[m, l], dst_ref=coming.at[m, l],
                send_sem=going_sem.at[m, l], recv_sem=coming_sem.at[m, l],
                device_id=(my_section, lax.rem(me + 1, part_count)), device_id_type=MESH,
            ).wait()

            def arrive(k, carry, l=l, now=now):
                table[now, 2 * tiles + k] = coming[m, l, k]
                return carry

            lax.fori_loop(0, others, arrive, 0)

            def quad(g, carry, l=l, now=now, later=later):
                parts = []
                for c in range(4):
                    at = (4 * g + c) * 4
                    pair = [
                        jnp.where(
                            low,
                            table[now, source_ref[l, at + 2 * h]],
                            table[now, source_ref[l, at + 2 * h + 1]],
                        )
                        for h in range(2)
                    ]
                    parts.append(jnp.concatenate(pair, axis=1))
                left = jnp.concatenate(parts, axis=0)
                summed = lax.dot_general(
                    left, held[l, g], (((1,), (1,)), ((), ())), preferred_element_type=jnp.float32
                )
                for t in range(2):
                    top = 2 * t * rows
                    cols = slice(t * lanes, (t + 1) * lanes)
                    pre_act = jnp.where(
                        low, summed[top : top + rows, cols], summed[top + rows : top + 2 * rows, cols]
                    )
                    pre_act = pre_act + bias_ref[l, 2 * g + t]
                    result = jnp.clip(pre_act, 0.0, 32.0)
                    if l == layer_count - 1:
                        outbox[m, 2 * g + t] = result.astype(jnp.bfloat16)
                    else:
                        table[later, 2 * (2 * g + t)] = result.astype(jnp.bfloat16)
                        table[later, 2 * (2 * g + t) + 1] = pltpu.roll(result, lanes // 2, 1).astype(jnp.bfloat16)
                return carry

            if l < layer_count - 1:
                lax.fori_loop(0, quads, quad, 0, unroll=4)
            else:
                for c in range(CHUNKS):
                    share = quads // CHUNKS
                    lax.fori_loop(c * share, (c + 1) * share, quad, 0, unroll=min(4, share))

                    @pl.when(my_section != last)
                    def _(c=c):
                        forward(m, c).start()

                    @pl.when((my_section == last) & (m != last))
                    def _(c=c):
                        deliver(m, c).start()

        return carry

    lax.fori_loop(0, micro_count, stage, 0)

    @pl.when(my_section == last)
    def _():
        own = pltpu.make_async_copy(outbox.at[last], out_ref, own_sem)
        own.start()
        own.wait()

    @pl.when(my_section != last)
    def _():
        for c in range(CHUNKS):
            deliver(0, c).wait_recv()

    @pl.when(my_section != 0)
    def _():
        for c in range(CHUNKS):
            feed(c).wait_send()

    def drain(m, carry):
        @pl.when((my_section != last) | (m != last))
        def _():
            for c in range(CHUNKS):
                forward(m, c).wait_send()

        return carry

    lax.fori_loop(0, micro_count, drain, 0)


def shards(images, weights, bias, pattern, counts):
    section_count = lax.axis_size("section")
    part_count = lax.axis_size("dom")
    my_part = lax.axis_index("dom")
    _, rows, width = images.shape
    layer_count, per_part, block_size, depth = weights.shape
    lanes = 2 * block_size
    tiles = width // lanes
    quads = per_part // 4
    others = part_count - 1
    micro_count = section_count * images.shape[0]
    wanted, source = prepare_tables(pattern, counts, per_part, part_count, my_part)
    tiled_images = images.reshape(rows, tiles, lanes).transpose(1, 0, 2)
    tiled_weights = weights.reshape(layer_count, quads, 4 * block_size, depth)
    tiled_bias = bias.astype(jnp.float32).reshape(layer_count, tiles, 1, lanes)
    in_vmem = pl.BlockSpec(memory_space=pltpu.VMEM)
    in_smem = pl.BlockSpec(memory_space=pltpu.SMEM)
    dma = pltpu.SemaphoreType.DMA
    flops = 2 * micro_count * layer_count * rows * per_part * block_size * depth
    result = pl.pallas_call(
        functools.partial(kernel, section_count, part_count),
        out_shape=jax.ShapeDtypeStruct((tiles, rows, lanes), jnp.bfloat16),
        in_specs=[in_smem, in_smem, in_vmem, pl.BlockSpec(memory_space=pl.ANY), in_vmem],
        out_specs=in_vmem,
        scratch_shapes=[
            pltpu.VMEM(tiled_weights.shape, jnp.bfloat16),
            pltpu.VMEM((micro_count, tiles, rows, lanes), jnp.bfloat16),
            pltpu.VMEM((micro_count, tiles, rows, lanes), jnp.bfloat16),
            pltpu.VMEM((2, 2 * tiles + part_count, rows, lanes), jnp.bfloat16),
            pltpu.VMEM((micro_count, layer_count, others, rows, lanes), jnp.bfloat16),
            pltpu.VMEM((micro_count, layer_count, others, rows, lanes), jnp.bfloat16),
            dma((layer_count,)),
            dma,
            dma((CHUNKS,)),
            dma((micro_count, CHUNKS)),
            dma((micro_count, CHUNKS)),
            dma((CHUNKS,)),
            dma((micro_count, layer_count)),
            dma((micro_count, layer_count)),
        ],
        compiler_params=pltpu.CompilerParams(
            collective_id=0, has_side_effects=True, vmem_limit_bytes=40 * 2**20
        ),
        cost_estimate=pl.CostEstimate(flops=flops, bytes_accessed=2 * weights.size, transcendentals=0),
    )(wanted, source, tiled_images, tiled_weights, tiled_bias)
    return result.transpose(1, 0, 2).reshape(1, rows, width)


def solution(mesh):
    placed = (
        P("section", None, "dom"),
        P("section", "dom", None, None),
        P("section", "dom"),
        P("section", None, None),
        P("section", "dom"),
    )
    return jax.shard_map(
        shards, mesh=mesh, in_specs=placed, out_specs=P("section", None, "dom"), check_vma=False
    )
```

```python
import functools

import jax
import jax.numpy as jnp
from jax import lax
from jax.experimental import pallas as pl
from jax.experimental.pallas import tpu as pltpu
from jax.sharding import PartitionSpec as P

MESH = pl.DeviceIdType.MESH
CHUNKS = 2
PIECE_ROWS = 16


def prepare_tables(pattern, counts, per_part, part_count, my_part):
    layer_count = pattern.shape[0]
    slot_count = pattern.shape[2]
    block_table = pattern.reshape(layer_count, part_count, per_part * slot_count)
    owners = block_table // per_part
    wanted = jnp.max(jnp.where(owners == my_part, block_table % per_part, 0), axis=2)
    own_rows = lax.dynamic_slice_in_dim(pattern, my_part * per_part, per_part, 1)
    own_owners = own_rows // per_part
    slots = jnp.arange(slot_count, dtype=jnp.int32)[None, None, :]
    local = (own_rows % per_part) ^ (slots & 1)
    remote = per_part + (my_part - own_owners + part_count) % part_count - 1
    source = jnp.where(own_owners == my_part, local, remote)
    source = jnp.where(slots < counts[:, :, None], source, per_part + part_count - 1)
    return wanted, source.reshape(layer_count, per_part * slot_count)


def kernel(
    section_count, part_count, halves, wanted_ref, source_ref, images_ref, weights_ref, bias_ref, out_ref,
    held, inbox, outbox, table, going, coming,
    weight_sem, own_sem, feed_sem, in_sem, out_sem, result_sem, going_sem, coming_sem, turn_sem,
):
    my_section = lax.axis_index("section")
    me = lax.axis_index("dom")
    layer_count, quads = weights_ref.shape[0], weights_ref.shape[1]
    piece_count, tiles, rows, lanes = inbox.shape
    per_chunk = tiles // CHUNKS
    share = quads // CHUNKS
    last = section_count - 1
    others = part_count - 1
    pieces = [(h, c) for h in range(halves) for c in range(CHUNKS)]

    loads = [
        pltpu.make_async_copy(weights_ref.at[l], held.at[l], weight_sem.at[l])
        for l in range(layer_count)
    ]
    for load in loads:
        load.start()

    barrier = pltpu.get_barrier_semaphore()

    def greet_part(step, carry):
        pl.semaphore_signal(
            barrier, inc=1, device_id=(my_section, lax.rem(me + step, part_count)), device_id_type=MESH
        )
        return carry

    def greet_section(step, carry):
        pl.semaphore_signal(
            barrier, inc=1, device_id=(lax.rem(my_section + step, section_count), me), device_id_type=MESH
        )
        return carry

    lax.fori_loop(1, part_count, greet_part, 0)
    lax.fori_loop(1, section_count, greet_section, 0)
    pl.semaphore_wait(barrier, others + section_count - 1)

    def chunk_of(c):
        return pl.ds(c * per_chunk, per_chunk)

    def feed(h, c):
        return pltpu.make_async_remote_copy(
            src_ref=images_ref.at[h, chunk_of(c)], dst_ref=inbox.at[my_section * halves + h, chunk_of(c)],
            send_sem=feed_sem.at[h, c], recv_sem=in_sem.at[my_section * halves + h, c],
            device_id=(0, me), device_id_type=MESH,
        )

    def forward(u, c):
        return pltpu.make_async_remote_copy(
            src_ref=outbox.at[u, chunk_of(c)], dst_ref=inbox.at[u, chunk_of(c)],
            send_sem=out_sem.at[u, c], recv_sem=in_sem.at[u, c],
            device_id=(lax.rem(my_section + 1, section_count), me), device_id_type=MESH,
        )

    def deliver(u, c):
        return pltpu.make_async_remote_copy(
            src_ref=outbox.at[u, chunk_of(c)], dst_ref=out_ref.at[lax.rem(u, halves), chunk_of(c)],
            send_sem=out_sem.at[u, c], recv_sem=result_sem.at[lax.rem(u, halves), c],
            device_id=(lax.div(u, halves), me), device_id_type=MESH,
        )

    @pl.when(my_section == 0)
    def _():
        own = pltpu.make_async_copy(images_ref, inbox.at[pl.ds(0, halves)], own_sem)
        own.start()
        own.wait()

    @pl.when(my_section > 1)
    def _():
        pl.semaphore_wait(turn_sem, 1)

    @pl.when(my_section != 0)
    def _():
        for h, c in pieces:
            feed(h, c).start()
        for h, c in pieces:
            feed(h, c).wait_send()

    @pl.when((my_section != 0) & (my_section != last))
    def _():
        pl.semaphore_signal(turn_sem, inc=1, device_id=(my_section + 1, me), device_id_type=MESH)

    low = lax.broadcasted_iota(jnp.int32, (rows, lanes), 1) < lanes // 2
    for l in range(layer_count):
        table[l, 2 * tiles + others] = jnp.zeros((rows, lanes), jnp.bfloat16)

    def turned(x):
        return pltpu.roll(x.astype(jnp.float32), lanes // 2, 1).astype(jnp.bfloat16)

    def exchange(u, l):
        return pltpu.make_async_remote_copy(
            src_ref=going.at[u, l], dst_ref=coming.at[u, l],
            send_sem=going_sem.at[u, l], recv_sem=coming_sem.at[u, l],
            device_id=(my_section, lax.rem(me + 1, part_count)), device_id_type=MESH,
        )

    def send(u, l):
        def one(step, carry):
            peer = lax.rem(me + step, part_count)
            block = wanted_ref[l, peer]
            going[u, l, step - 1] = jnp.where(low, table[l, block], table[l, block ^ 1])
            pltpu.make_async_remote_copy(
                src_ref=going.at[u, l, step - 1], dst_ref=coming.at[u, l, step - 1],
                send_sem=going_sem.at[u, l], recv_sem=coming_sem.at[u, l],
                device_id=(my_section, peer), device_id_type=MESH,
            ).start()
            return carry

        lax.fori_loop(1, part_count, one, 0)

    def enter(u):
        def tile(q, carry):
            x = inbox[u, q]
            table[0, 2 * q] = x
            table[0, 2 * q + 1] = turned(x)
            return carry

        @pl.when((my_section != 0) | (u >= halves))
        def _():
            for c in range(CHUNKS):
                forward(u, c).wait_recv()

        lax.fori_loop(0, tiles, tile, 0, unroll=8)
        send(u, 0)

    def layer(u, l):
        exchange(u, l).wait()

        def arrive(k, carry):
            table[l, 2 * tiles + k] = coming[u, l, k]
            return carry

        lax.fori_loop(0, others, arrive, 0)

        def quad(g, carry):
            parts = []
            for c in range(4):
                at = (4 * g + c) * 4
                pair = [
                    jnp.where(
                        low,
                        table[l, source_ref[l, at + 2 * h]],
                        table[l, source_ref[l, at + 2 * h + 1]],
                    )
                    for h in range(2)
                ]
                parts.append(jnp.concatenate(pair, axis=1))
            left = jnp.concatenate(parts, axis=0)
            summed = lax.dot_general(
                left, held[l, g], (((1,), (0,)), ((), ())), preferred_element_type=jnp.float32
            )
            for t in range(2):
                top = 2 * t * rows
                cols = slice(t * lanes, (t + 1) * lanes)
                pre_act = jnp.where(
                    low, summed[top : top + rows, cols], summed[top + rows : top + 2 * rows, cols]
                )
                pre_act = pre_act + bias_ref[l, 2 * g + t]
                result = jnp.clip(pre_act, 0.0, 32.0)
                if l == layer_count - 1:
                    outbox[u, 2 * g + t] = result.astype(jnp.bfloat16)
                else:
                    table[l + 1, 2 * (2 * g + t)] = result.astype(jnp.bfloat16)
                    table[l + 1, 2 * (2 * g + t) + 1] = pltpu.roll(result, lanes // 2, 1).astype(jnp.bfloat16)
            return carry

        if l < layer_count - 1:
            lax.fori_loop(0, quads, quad, 0, unroll=min(8, quads))
            send(u, l + 1)
        else:
            for c in range(CHUNKS):
                lax.fori_loop(c * share, (c + 1) * share, quad, 0, unroll=min(8, share))

                @pl.when(my_section != last)
                def _(c=c):
                    forward(u, c).start()

                @pl.when((my_section == last) & (u < last * halves))
                def _(c=c):
                    deliver(u, c).start()

    for l, load in enumerate(loads):
        load.wait()

        def flip(g, carry, l=l):
            held[l, g] = held[l, g].T
            return carry

        lax.fori_loop(0, quads, flip, 0)
    enter(0)

    def stage(u, carry):
        for l in range(layer_count):
            layer(u, l)
            if l == 0:

                @pl.when(u + 1 < piece_count)
                def _():
                    enter(u + 1)

        return carry

    lax.fori_loop(0, piece_count, stage, 0)

    @pl.when(my_section == last)
    def _():
        own = pltpu.make_async_copy(outbox.at[pl.ds(last * halves, halves)], out_ref, own_sem)
        own.start()
        own.wait()

    @pl.when(my_section != last)
    def _():
        for h, c in pieces:
            deliver(h, c).wait_recv()

    def drain(u, carry):
        @pl.when((my_section != last) | (u < last * halves))
        def _():
            for c in range(CHUNKS):
                forward(u, c).wait_send()

        return carry

    lax.fori_loop(0, piece_count, drain, 0)


def shards(images, weights, bias, pattern, counts):
    section_count = lax.axis_size("section")
    part_count = lax.axis_size("dom")
    my_part = lax.axis_index("dom")
    _, rows, width = images.shape
    layer_count, per_part, block_size, depth = weights.shape
    lanes = 2 * block_size
    halves = rows // PIECE_ROWS
    tiles = width // lanes
    quads = per_part // 4
    others = part_count - 1
    piece_count = section_count * halves
    wanted, source = prepare_tables(pattern, counts, per_part, part_count, my_part)
    tiled_images = images.reshape(halves, PIECE_ROWS, tiles, lanes).transpose(0, 2, 1, 3)
    tiled_weights = weights.reshape(layer_count, quads, 4 * block_size, depth)
    tiled_bias = bias.astype(jnp.float32).reshape(layer_count, tiles, 1, lanes)
    in_vmem = pl.BlockSpec(memory_space=pltpu.VMEM)
    in_smem = pl.BlockSpec(memory_space=pltpu.SMEM)
    dma = pltpu.SemaphoreType.DMA
    flops = 2 * section_count * layer_count * rows * per_part * block_size * depth
    result = pl.pallas_call(
        functools.partial(kernel, section_count, part_count, halves),
        out_shape=jax.ShapeDtypeStruct((halves, tiles, PIECE_ROWS, lanes), jnp.bfloat16),
        in_specs=[in_smem, in_smem, in_vmem, pl.BlockSpec(memory_space=pl.ANY), in_vmem],
        out_specs=in_vmem,
        scratch_shapes=[
            pltpu.VMEM(tiled_weights.shape, jnp.bfloat16),
            pltpu.VMEM((piece_count, tiles, PIECE_ROWS, lanes), jnp.bfloat16),
            pltpu.VMEM((piece_count, tiles, PIECE_ROWS, lanes), jnp.bfloat16),
            pltpu.VMEM((layer_count, 2 * tiles + part_count, PIECE_ROWS, lanes), jnp.bfloat16),
            pltpu.VMEM((piece_count, layer_count, others, PIECE_ROWS, lanes), jnp.bfloat16),
            pltpu.VMEM((piece_count, layer_count, others, PIECE_ROWS, lanes), jnp.bfloat16),
            dma((layer_count,)),
            dma,
            dma((halves, CHUNKS)),
            dma((piece_count, CHUNKS)),
            dma((piece_count, CHUNKS)),
            dma((halves, CHUNKS)),
            dma((piece_count, layer_count)),
            dma((piece_count, layer_count)),
            pltpu.SemaphoreType.REGULAR,
        ],
        compiler_params=pltpu.CompilerParams(
            collective_id=0, has_side_effects=True, vmem_limit_bytes=40 * 2**20
        ),
        cost_estimate=pl.CostEstimate(flops=flops, bytes_accessed=2 * weights.size, transcendentals=0),
    )(wanted, source, tiled_images, tiled_weights, tiled_bias)
    return result.transpose(0, 2, 1, 3).reshape(1, rows, width)


def solution(mesh):
    placed = (
        P("section", None, "dom"),
        P("section", "dom", None, None),
        P("section", "dom"),
        P("section", None, None),
        P("section", "dom"),
    )
    return jax.shard_map(
        shards, mesh=mesh, in_specs=placed, out_specs=P("section", None, "dom"), check_vma=False
    )
```

```python
import functools

import jax
import jax.numpy as jnp
from jax import lax
from jax.experimental import pallas as pl
from jax.experimental.pallas import tpu as pltpu
from jax.sharding import PartitionSpec as P

MESH = pl.DeviceIdType.MESH
CHUNKS = 2
PIECE_ROWS = 16


def prepare_tables(pattern, counts, per_part, part_count, my_part):
    layer_count = pattern.shape[0]
    slot_count = pattern.shape[2]
    block_table = pattern.reshape(layer_count, part_count, per_part * slot_count)
    owners = block_table // per_part
    wanted = jnp.max(jnp.where(owners == my_part, block_table % per_part, 0), axis=2)
    own_rows = lax.dynamic_slice_in_dim(pattern, my_part * per_part, per_part, 1)
    own_owners = own_rows // per_part
    slots = jnp.arange(slot_count, dtype=jnp.int32)[None, None, :]
    local = (own_rows % per_part) ^ (slots & 1)
    remote = per_part + (my_part - own_owners + part_count) % part_count - 1
    source = jnp.where(own_owners == my_part, local, remote)
    source = jnp.where(slots < counts[:, :, None], source, per_part + part_count - 1)
    return wanted, source.reshape(layer_count, per_part * slot_count)


def kernel(
    section_count, part_count, halves, wanted_ref, source_ref, images_ref, weights_ref, bias_ref, out_ref,
    held, inbox, outbox, going, coming,
    weight_sem, own_sem, feed_sem, in_sem, out_sem, result_sem, going_sem, coming_sem, turn_sem, *tables,
):
    my_section = lax.axis_index("section")
    me = lax.axis_index("dom")
    layer_count, quads = weights_ref.shape[0], weights_ref.shape[1]
    piece_count, tiles, rows, lanes = inbox.shape
    per_chunk = tiles // CHUNKS
    share = quads // CHUNKS
    last = section_count - 1
    others = part_count - 1
    pieces = [(h, c) for h in range(halves) for c in range(CHUNKS)]

    loads = [
        pltpu.make_async_copy(weights_ref.at[l], held.at[l], weight_sem.at[l])
        for l in range(layer_count)
    ]
    for load in loads:
        load.start()

    barrier = pltpu.get_barrier_semaphore()

    def greet_part(step, carry):
        pl.semaphore_signal(
            barrier, inc=1, device_id=(my_section, lax.rem(me + step, part_count)), device_id_type=MESH
        )
        return carry

    def greet_section(step, carry):
        pl.semaphore_signal(
            barrier, inc=1, device_id=(lax.rem(my_section + step, section_count), me), device_id_type=MESH
        )
        return carry

    lax.fori_loop(1, part_count, greet_part, 0)
    lax.fori_loop(1, section_count, greet_section, 0)
    pl.semaphore_wait(barrier, others + section_count - 1)

    def chunk_of(c):
        return pl.ds(c * per_chunk, per_chunk)

    def feed(h, c):
        return pltpu.make_async_remote_copy(
            src_ref=images_ref.at[h, chunk_of(c)], dst_ref=inbox.at[my_section * halves + h, chunk_of(c)],
            send_sem=feed_sem.at[h, c], recv_sem=in_sem.at[my_section * halves + h, c],
            device_id=(0, me), device_id_type=MESH,
        )

    def forward(u, c):
        return pltpu.make_async_remote_copy(
            src_ref=outbox.at[u, chunk_of(c)], dst_ref=inbox.at[u, chunk_of(c)],
            send_sem=out_sem.at[u, c], recv_sem=in_sem.at[u, c],
            device_id=(lax.rem(my_section + 1, section_count), me), device_id_type=MESH,
        )

    def deliver(u, c):
        return pltpu.make_async_remote_copy(
            src_ref=outbox.at[u, chunk_of(c)], dst_ref=out_ref.at[lax.rem(u, halves), chunk_of(c)],
            send_sem=out_sem.at[u, c], recv_sem=result_sem.at[lax.rem(u, halves), c],
            device_id=(lax.div(u, halves), me), device_id_type=MESH,
        )

    @pl.when(my_section == 0)
    def _():
        own = pltpu.make_async_copy(images_ref, inbox.at[pl.ds(0, halves)], own_sem)
        own.start()
        own.wait()

    @pl.when(my_section > 1)
    def _():
        pl.semaphore_wait(turn_sem, 1)

    @pl.when(my_section != 0)
    def _():
        for h, c in pieces:
            feed(h, c).start()
        for h, c in pieces:
            feed(h, c).wait_send()

    @pl.when((my_section != 0) & (my_section != last))
    def _():
        pl.semaphore_signal(turn_sem, inc=1, device_id=(my_section + 1, me), device_id_type=MESH)

    low = lax.broadcasted_iota(jnp.int32, (rows, lanes), 1) < lanes // 2
    for l in range(layer_count):
        tables[l][2 * tiles + others] = jnp.zeros((rows, lanes), jnp.bfloat16)

    def turned(x):
        return pltpu.roll(x.astype(jnp.float32), lanes // 2, 1).astype(jnp.bfloat16)

    def exchange(u, l):
        return pltpu.make_async_remote_copy(
            src_ref=going.at[u, l], dst_ref=coming.at[u, l],
            send_sem=going_sem.at[u, l], recv_sem=coming_sem.at[u, l],
            device_id=(my_section, lax.rem(me + 1, part_count)), device_id_type=MESH,
        )

    def send(u, l):
        def one(step, carry):
            peer = lax.rem(me + step, part_count)
            block = wanted_ref[l, peer]
            going[u, l, step - 1] = jnp.where(low, tables[l][block], tables[l][block ^ 1])
            pltpu.make_async_remote_copy(
                src_ref=going.at[u, l, step - 1], dst_ref=coming.at[u, l, step - 1],
                send_sem=going_sem.at[u, l], recv_sem=coming_sem.at[u, l],
                device_id=(my_section, peer), device_id_type=MESH,
            ).start()
            return carry

        lax.fori_loop(1, part_count, one, 0, unroll=min(7, others))

    def enter(u):
        def tile(q, carry):
            x = inbox[u, q]
            tables[0][2 * q] = x
            tables[0][2 * q + 1] = turned(x)
            return carry

        @pl.when((my_section != 0) | (u >= halves))
        def _():
            for c in range(CHUNKS):
                forward(u, c).wait_recv()

        lax.fori_loop(0, tiles, tile, 0, unroll=8)
        send(u, 0)

    def layer(u, l):
        exchange(u, l).wait()

        def arrive(k, carry):
            tables[l][2 * tiles + k] = coming[u, l, k]
            return carry

        lax.fori_loop(0, others, arrive, 0, unroll=min(7, others))

        def quad(g, carry):
            parts = []
            for c in range(4):
                at = (4 * g + c) * 4
                pair = [
                    jnp.where(
                        low,
                        tables[l][source_ref[l, at + 2 * h]],
                        tables[l][source_ref[l, at + 2 * h + 1]],
                    )
                    for h in range(2)
                ]
                parts.append(jnp.concatenate(pair, axis=1))
            left = jnp.concatenate(parts, axis=0)
            summed = lax.dot_general(
                left, held[l, g], (((1,), (1,)), ((), ())), preferred_element_type=jnp.float32
            )
            for t in range(2):
                top = 2 * t * rows
                cols = slice(t * lanes, (t + 1) * lanes)
                pre_act = jnp.where(
                    low, summed[top : top + rows, cols], summed[top + rows : top + 2 * rows, cols]
                )
                pre_act = pre_act + bias_ref[l, 2 * g + t]
                result = jnp.clip(pre_act, 0.0, 32.0)
                if l == layer_count - 1:
                    outbox[u, 2 * g + t] = result.astype(jnp.bfloat16)
                else:
                    tables[l + 1][2 * (2 * g + t)] = result.astype(jnp.bfloat16)
                    tables[l + 1][2 * (2 * g + t) + 1] = pltpu.roll(result, lanes // 2, 1).astype(jnp.bfloat16)
            return carry

        if l < layer_count - 1:
            lax.fori_loop(0, quads, quad, 0, unroll=min(8, quads))
            send(u, l + 1)
        else:
            for c in range(CHUNKS):
                lax.fori_loop(c * share, (c + 1) * share, quad, 0, unroll=min(8, share))

                @pl.when(my_section != last)
                def _(c=c):
                    forward(u, c).start()

                @pl.when((my_section == last) & (u < last * halves))
                def _(c=c):
                    deliver(u, c).start()

    enter(0)
    for load in loads:
        load.wait()

    def stage(u, carry):
        for l in range(layer_count):
            layer(u, l)
            if l == 0:

                @pl.when(u + 1 < piece_count)
                def _():
                    enter(u + 1)

        return carry

    lax.fori_loop(0, piece_count, stage, 0)

    @pl.when(my_section == last)
    def _():
        own = pltpu.make_async_copy(outbox.at[pl.ds(last * halves, halves)], out_ref, own_sem)
        own.start()
        own.wait()

    @pl.when(my_section != last)
    def _():
        for h, c in pieces:
            deliver(h, c).wait_recv()

    def drain(u, carry):
        @pl.when((my_section != last) | (u < last * halves))
        def _():
            for c in range(CHUNKS):
                forward(u, c).wait_send()

        return carry

    lax.fori_loop(0, piece_count, drain, 0)


def shards(images, weights, bias, pattern, counts):
    section_count = lax.axis_size("section")
    part_count = lax.axis_size("dom")
    my_part = lax.axis_index("dom")
    _, rows, width = images.shape
    layer_count, per_part, block_size, depth = weights.shape
    lanes = 2 * block_size
    halves = rows // PIECE_ROWS
    tiles = width // lanes
    quads = per_part // 4
    others = part_count - 1
    piece_count = section_count * halves
    wanted, source = prepare_tables(pattern, counts, per_part, part_count, my_part)
    tiled_images = images.reshape(halves, PIECE_ROWS, tiles, lanes).transpose(0, 2, 1, 3)
    tiled_weights = weights.reshape(layer_count, quads, 4 * block_size, depth)
    tiled_bias = bias.astype(jnp.float32).reshape(layer_count, tiles, 1, lanes)
    in_vmem = pl.BlockSpec(memory_space=pltpu.VMEM)
    in_smem = pl.BlockSpec(memory_space=pltpu.SMEM)
    dma = pltpu.SemaphoreType.DMA
    flops = 2 * section_count * layer_count * rows * per_part * block_size * depth
    result = pl.pallas_call(
        functools.partial(kernel, section_count, part_count, halves),
        out_shape=jax.ShapeDtypeStruct((halves, tiles, PIECE_ROWS, lanes), jnp.bfloat16),
        in_specs=[in_smem, in_smem, in_vmem, pl.BlockSpec(memory_space=pl.ANY), in_vmem],
        out_specs=in_vmem,
        scratch_shapes=[
            pltpu.VMEM(tiled_weights.shape, jnp.bfloat16),
            pltpu.VMEM((piece_count, tiles, PIECE_ROWS, lanes), jnp.bfloat16),
            pltpu.VMEM((piece_count, tiles, PIECE_ROWS, lanes), jnp.bfloat16),
            pltpu.VMEM((piece_count, layer_count, others, PIECE_ROWS, lanes), jnp.bfloat16),
            pltpu.VMEM((piece_count, layer_count, others, PIECE_ROWS, lanes), jnp.bfloat16),
            dma((layer_count,)),
            dma,
            dma((halves, CHUNKS)),
            dma((piece_count, CHUNKS)),
            dma((piece_count, CHUNKS)),
            dma((halves, CHUNKS)),
            dma((piece_count, layer_count)),
            dma((piece_count, layer_count)),
            pltpu.SemaphoreType.REGULAR,
        ]
        + [pltpu.VMEM((2 * tiles + part_count, PIECE_ROWS, lanes), jnp.bfloat16)] * layer_count,
        compiler_params=pltpu.CompilerParams(
            collective_id=0, has_side_effects=True, vmem_limit_bytes=58 * 2**20
        ),
        cost_estimate=pl.CostEstimate(flops=flops, bytes_accessed=2 * weights.size, transcendentals=0),
    )(wanted, source, tiled_images, tiled_weights, tiled_bias)
    return result.transpose(0, 2, 1, 3).reshape(1, rows, width)


def solution(mesh):
    placed = (
        P("section", None, "dom"),
        P("section", "dom", None, None),
        P("section", "dom"),
        P("section", None, None),
        P("section", "dom"),
    )
    return jax.shard_map(
        shards, mesh=mesh, in_specs=placed, out_specs=P("section", None, "dom"), check_vma=False
    )
```

```python
import functools

import jax
import jax.numpy as jnp
from jax import lax
from jax.experimental import pallas as pl
from jax.experimental.pallas import tpu as pltpu
from jax.sharding import PartitionSpec as P

MESH = pl.DeviceIdType.MESH
CHUNKS = 4
PIECE_ROWS = 16


def prepare_tables(pattern, counts, per_part, part_count, my_part):
    layer_count = pattern.shape[0]
    slot_count = pattern.shape[2]
    block_table = pattern.reshape(layer_count, part_count, per_part * slot_count)
    owners = block_table // per_part
    wanted = jnp.max(jnp.where(owners == my_part, block_table % per_part, 0), axis=2)
    own_rows = lax.dynamic_slice_in_dim(pattern, my_part * per_part, per_part, 1)
    own_owners = own_rows // per_part
    slots = jnp.arange(slot_count, dtype=jnp.int32)[None, None, :]
    local = (own_rows % per_part) ^ (slots & 1)
    remote = per_part + (my_part - own_owners + part_count) % part_count - 1
    source = jnp.where(own_owners == my_part, local, remote)
    source = jnp.where(slots < counts[:, :, None], source, per_part + part_count - 1)
    return wanted, source.reshape(layer_count, per_part * slot_count)


def kernel(
    section_count, part_count, halves, wanted_ref, source_ref, images_ref, weights_ref, bias_ref, out_ref,
    held, flipped, inbox, outbox, going, coming,
    weight_sem, own_sem, feed_sem, in_sem, out_sem, result_sem, going_sem, coming_sem, turn_sem, *tables,
):
    my_section = lax.axis_index("section")
    me = lax.axis_index("dom")
    layer_count, quads = weights_ref.shape[0], weights_ref.shape[1]
    piece_count, tiles, rows, lanes = inbox.shape
    per_chunk = tiles // CHUNKS
    share = quads // CHUNKS
    last = section_count - 1
    others = part_count - 1
    pieces = [(h, c) for h in range(halves) for c in range(CHUNKS)]

    loads = [
        pltpu.make_async_copy(weights_ref.at[l], held.at[l], weight_sem.at[l])
        for l in range(layer_count)
    ]
    for load in loads:
        load.start()

    barrier = pltpu.get_barrier_semaphore()

    def greet_part(step, carry):
        pl.semaphore_signal(
            barrier, inc=1, device_id=(my_section, lax.rem(me + step, part_count)), device_id_type=MESH
        )
        return carry

    def greet_section(step, carry):
        pl.semaphore_signal(
            barrier, inc=1, device_id=(lax.rem(my_section + step, section_count), me), device_id_type=MESH
        )
        return carry

    lax.fori_loop(1, part_count, greet_part, 0)
    lax.fori_loop(1, section_count, greet_section, 0)
    pl.semaphore_wait(barrier, others + section_count - 1)

    def chunk_of(c):
        return pl.ds(c * per_chunk, per_chunk)

    def feed(h, c):
        return pltpu.make_async_remote_copy(
            src_ref=images_ref.at[h, chunk_of(c)], dst_ref=inbox.at[my_section * halves + h, chunk_of(c)],
            send_sem=feed_sem.at[h, c], recv_sem=in_sem.at[my_section * halves + h, c],
            device_id=(0, me), device_id_type=MESH,
        )

    def forward(u, c):
        return pltpu.make_async_remote_copy(
            src_ref=outbox.at[u, chunk_of(c)], dst_ref=inbox.at[u, chunk_of(c)],
            send_sem=out_sem.at[u, c], recv_sem=in_sem.at[u, c],
            device_id=(lax.rem(my_section + 1, section_count), me), device_id_type=MESH,
        )

    def deliver(u, c):
        return pltpu.make_async_remote_copy(
            src_ref=outbox.at[u, chunk_of(c)], dst_ref=out_ref.at[lax.rem(u, halves), chunk_of(c)],
            send_sem=out_sem.at[u, c], recv_sem=result_sem.at[lax.rem(u, halves), c],
            device_id=(lax.div(u, halves), me), device_id_type=MESH,
        )

    @pl.when(my_section == 0)
    def _():
        own = pltpu.make_async_copy(images_ref, inbox.at[pl.ds(0, halves)], own_sem)
        own.start()
        own.wait()

    @pl.when(my_section > 1)
    def _():
        pl.semaphore_wait(turn_sem, 1)

    @pl.when(my_section != 0)
    def _():
        for h, c in pieces:
            feed(h, c).start()
        for h, c in pieces:
            feed(h, c).wait_send()

    @pl.when((my_section != 0) & (my_section != last))
    def _():
        pl.semaphore_signal(turn_sem, inc=1, device_id=(my_section + 1, me), device_id_type=MESH)

    low = lax.broadcasted_iota(jnp.int32, (rows, lanes), 1) < lanes // 2
    for l in range(layer_count):
        tables[l][2 * tiles + others] = jnp.zeros((rows, lanes), jnp.bfloat16)

    def turned(x):
        return pltpu.roll(x.astype(jnp.float32), lanes // 2, 1).astype(jnp.bfloat16)

    def exchange(u, l):
        return pltpu.make_async_remote_copy(
            src_ref=going.at[u, l], dst_ref=coming.at[u, l],
            send_sem=going_sem.at[u, l], recv_sem=coming_sem.at[u, l],
            device_id=(my_section, lax.rem(me + 1, part_count)), device_id_type=MESH,
        )

    def send(u, l):
        def one(step, carry):
            peer = lax.rem(me + step, part_count)
            block = wanted_ref[l, peer]
            going[u, l, step - 1] = jnp.where(low, tables[l][block], tables[l][block ^ 1])
            pltpu.make_async_remote_copy(
                src_ref=going.at[u, l, step - 1], dst_ref=coming.at[u, l, step - 1],
                send_sem=going_sem.at[u, l], recv_sem=coming_sem.at[u, l],
                device_id=(my_section, peer), device_id_type=MESH,
            ).start()
            return carry

        lax.fori_loop(1, part_count, one, 0, unroll=min(7, others))

    def enter(u):
        def tile(q, carry):
            x = inbox[u, q]
            tables[0][2 * q] = x
            tables[0][2 * q + 1] = turned(x)
            return carry

        @pl.when((my_section != 0) | (u >= halves))
        def _():
            for c in range(CHUNKS):
                forward(u, c).wait_recv()

        lax.fori_loop(0, tiles, tile, 0, unroll=8)
        send(u, 0)

    def layer(u, l):
        exchange(u, l).wait()

        def arrive(k, carry):
            tables[l][2 * tiles + k] = coming[u, l, k]
            return carry

        lax.fori_loop(0, others, arrive, 0, unroll=min(7, others))

        def quad(g, carry):
            parts = []
            for c in range(4):
                at = (4 * g + c) * 4
                pair = [
                    jnp.where(
                        low,
                        tables[l][source_ref[l, at + 2 * h]],
                        tables[l][source_ref[l, at + 2 * h + 1]],
                    )
                    for h in range(2)
                ]
                parts.append(jnp.concatenate(pair, axis=1))
            left = jnp.concatenate(parts, axis=0)
            summed = lax.dot_general(
                left, flipped[l, g], (((1,), (0,)), ((), ())), preferred_element_type=jnp.float32
            )
            for t in range(2):
                top = 2 * t * rows
                cols = slice(t * lanes, (t + 1) * lanes)
                pre_act = jnp.where(
                    low, summed[top : top + rows, cols], summed[top + rows : top + 2 * rows, cols]
                )
                pre_act = pre_act + bias_ref[l, 2 * g + t]
                result = jnp.clip(pre_act, 0.0, 32.0)
                if l == layer_count - 1:
                    outbox[u, 2 * g + t] = result.astype(jnp.bfloat16)
                else:
                    tables[l + 1][2 * (2 * g + t)] = result.astype(jnp.bfloat16)
                    tables[l + 1][2 * (2 * g + t) + 1] = pltpu.roll(result, lanes // 2, 1).astype(jnp.bfloat16)
            return carry

        if l < layer_count - 1:
            lax.fori_loop(0, quads, quad, 0, unroll=min(8, quads))
            send(u, l + 1)
        else:
            for c in range(CHUNKS):
                lax.fori_loop(c * share, (c + 1) * share, quad, 0, unroll=min(8, share))

                @pl.when(my_section != last)
                def _(c=c):
                    forward(u, c).start()

                @pl.when((my_section == last) & (u < last * halves))
                def _(c=c):
                    deliver(u, c).start()

    for l, load in enumerate(loads):
        load.wait()

        def flip(g, carry, l=l):
            flipped[l, g] = held[l, g].T
            return carry

        lax.fori_loop(0, quads, flip, 0, unroll=min(4, quads))
    enter(0)

    def stage(u, carry):
        for l in range(layer_count):
            layer(u, l)
            if l == 0:

                @pl.when(u + 1 < piece_count)
                def _():
                    enter(u + 1)

        return carry

    lax.fori_loop(0, piece_count, stage, 0)

    @pl.when(my_section == last)
    def _():
        own = pltpu.make_async_copy(outbox.at[pl.ds(last * halves, halves)], out_ref, own_sem)
        own.start()
        own.wait()

    @pl.when(my_section != last)
    def _():
        for h, c in pieces:
            deliver(h, c).wait_recv()

    def drain(u, carry):
        @pl.when((my_section != last) | (u < last * halves))
        def _():
            for c in range(CHUNKS):
                forward(u, c).wait_send()

        return carry

    lax.fori_loop(0, piece_count, drain, 0)


def shards(images, weights, bias, pattern, counts):
    section_count = lax.axis_size("section")
    part_count = lax.axis_size("dom")
    my_part = lax.axis_index("dom")
    _, rows, width = images.shape
    layer_count, per_part, block_size, depth = weights.shape
    lanes = 2 * block_size
    halves = rows // PIECE_ROWS
    tiles = width // lanes
    quads = per_part // 4
    others = part_count - 1
    piece_count = section_count * halves
    wanted, source = prepare_tables(pattern, counts, per_part, part_count, my_part)
    tiled_images = images.reshape(halves, PIECE_ROWS, tiles, lanes).transpose(0, 2, 1, 3)
    tiled_weights = weights.reshape(layer_count, quads, 4 * block_size, depth)
    tiled_bias = bias.astype(jnp.float32).reshape(layer_count, tiles, 1, lanes)
    in_vmem = pl.BlockSpec(memory_space=pltpu.VMEM)
    in_smem = pl.BlockSpec(memory_space=pltpu.SMEM)
    dma = pltpu.SemaphoreType.DMA
    flops = 2 * section_count * layer_count * rows * per_part * block_size * depth
    result = pl.pallas_call(
        functools.partial(kernel, section_count, part_count, halves),
        out_shape=jax.ShapeDtypeStruct((halves, tiles, PIECE_ROWS, lanes), jnp.bfloat16),
        in_specs=[in_smem, in_smem, in_vmem, pl.BlockSpec(memory_space=pl.ANY), in_vmem],
        out_specs=in_vmem,
        scratch_shapes=[
            pltpu.VMEM(tiled_weights.shape, jnp.bfloat16),
            pltpu.VMEM((layer_count, quads, depth, 4 * block_size), jnp.bfloat16),
            pltpu.VMEM((piece_count, tiles, PIECE_ROWS, lanes), jnp.bfloat16),
            pltpu.VMEM((piece_count, tiles, PIECE_ROWS, lanes), jnp.bfloat16),
            pltpu.VMEM((piece_count, layer_count, others, PIECE_ROWS, lanes), jnp.bfloat16),
            pltpu.VMEM((piece_count, layer_count, others, PIECE_ROWS, lanes), jnp.bfloat16),
            dma((layer_count,)),
            dma,
            dma((halves, CHUNKS)),
            dma((piece_count, CHUNKS)),
            dma((piece_count, CHUNKS)),
            dma((halves, CHUNKS)),
            dma((piece_count, layer_count)),
            dma((piece_count, layer_count)),
            pltpu.SemaphoreType.REGULAR,
        ]
        + [pltpu.VMEM((2 * tiles + part_count, PIECE_ROWS, lanes), jnp.bfloat16)] * layer_count,
        compiler_params=pltpu.CompilerParams(
            collective_id=0, has_side_effects=True, vmem_limit_bytes=58 * 2**20
        ),
        cost_estimate=pl.CostEstimate(flops=flops, bytes_accessed=2 * weights.size, transcendentals=0),
    )(wanted, source, tiled_images, tiled_weights, tiled_bias)
    return result.transpose(0, 2, 1, 3).reshape(1, rows, width)


def solution(mesh):
    placed = (
        P("section", None, "dom"),
        P("section", "dom", None, None),
        P("section", "dom"),
        P("section", None, None),
        P("section", "dom"),
    )
    return jax.shard_map(
        shards, mesh=mesh, in_specs=placed, out_specs=P("section", None, "dom"), check_vma=False
    )
```

```python
import functools

import jax
import jax.numpy as jnp
from jax import lax
from jax.experimental import pallas as pl
from jax.experimental.pallas import tpu as pltpu
from jax.sharding import PartitionSpec as P

MESH = pl.DeviceIdType.MESH
CHUNKS = 4
PIECE_ROWS = 16


def prepare_tables(pattern, counts, per_part, part_count, my_part):
    layer_count = pattern.shape[0]
    slot_count = pattern.shape[2]
    block_table = pattern.reshape(layer_count, part_count, per_part * slot_count)
    owners = block_table // per_part
    wanted = jnp.max(jnp.where(owners == my_part, block_table % per_part, 0), axis=2)
    own_rows = lax.dynamic_slice_in_dim(pattern, my_part * per_part, per_part, 1)
    own_owners = own_rows // per_part
    slots = jnp.arange(slot_count, dtype=jnp.int32)[None, None, :]
    local = (own_rows % per_part) ^ (slots & 1)
    remote = per_part + (my_part - own_owners + part_count) % part_count - 1
    source = jnp.where(own_owners == my_part, local, remote)
    source = jnp.where(slots < counts[:, :, None], source, per_part + part_count - 1)
    return wanted, source.reshape(layer_count, per_part * slot_count)


def kernel(
    section_count, part_count, halves, wanted_ref, source_ref, images_ref, weights_ref, bias_ref, out_ref,
    held, flipped, inbox, outbox, going, coming,
    weight_sem, own_sem, feed_sem, in_sem, out_sem, result_sem, going_sem, coming_sem, turn_sem, *tables,
):
    my_section = lax.axis_index("section")
    me = lax.axis_index("dom")
    layer_count, quads = weights_ref.shape[0], weights_ref.shape[1]
    piece_count, tiles, rows, lanes = inbox.shape
    per_chunk = tiles // CHUNKS
    share = quads // CHUNKS
    last = section_count - 1
    others = part_count - 1
    pieces = [(h, c) for h in range(halves) for c in range(CHUNKS)]

    loads = [
        pltpu.make_async_copy(weights_ref.at[l], held.at[l], weight_sem.at[l])
        for l in range(layer_count)
    ]
    for load in loads:
        load.start()

    barrier = pltpu.get_barrier_semaphore()

    def greet_part(step, carry):
        pl.semaphore_signal(
            barrier, inc=1, device_id=(my_section, lax.rem(me + step, part_count)), device_id_type=MESH
        )
        return carry

    def greet_section(step, carry):
        pl.semaphore_signal(
            barrier, inc=1, device_id=(lax.rem(my_section + step, section_count), me), device_id_type=MESH
        )
        return carry

    lax.fori_loop(1, part_count, greet_part, 0)
    lax.fori_loop(1, section_count, greet_section, 0)
    pl.semaphore_wait(barrier, others + section_count - 1)

    def chunk_of(c):
        return pl.ds(c * per_chunk, per_chunk)

    def feed(h, c):
        return pltpu.make_async_remote_copy(
            src_ref=images_ref.at[h, chunk_of(c)], dst_ref=inbox.at[my_section * halves + h, chunk_of(c)],
            send_sem=feed_sem.at[h, c], recv_sem=in_sem.at[my_section * halves + h, c],
            device_id=(0, me), device_id_type=MESH,
        )

    def forward(u, c):
        return pltpu.make_async_remote_copy(
            src_ref=outbox.at[u, chunk_of(c)], dst_ref=inbox.at[u, chunk_of(c)],
            send_sem=out_sem.at[u, c], recv_sem=in_sem.at[u, c],
            device_id=(lax.rem(my_section + 1, section_count), me), device_id_type=MESH,
        )

    def deliver(u, c):
        return pltpu.make_async_remote_copy(
            src_ref=outbox.at[u, chunk_of(c)], dst_ref=out_ref.at[lax.rem(u, halves), chunk_of(c)],
            send_sem=out_sem.at[u, c], recv_sem=result_sem.at[lax.rem(u, halves), c],
            device_id=(lax.div(u, halves), me), device_id_type=MESH,
        )

    @pl.when(my_section == 0)
    def _():
        own = pltpu.make_async_copy(images_ref, inbox.at[pl.ds(0, halves)], own_sem)
        own.start()
        own.wait()

    @pl.when(my_section > 1)
    def _():
        pl.semaphore_wait(turn_sem, 1)

    @pl.when(my_section != 0)
    def _():
        for h, c in pieces:
            feed(h, c).start()
        for h, c in pieces:
            feed(h, c).wait_send()

    @pl.when((my_section != 0) & (my_section != last))
    def _():
        pl.semaphore_signal(turn_sem, inc=1, device_id=(my_section + 1, me), device_id_type=MESH)

    low = lax.broadcasted_iota(jnp.int32, (rows, lanes), 1) < lanes // 2
    for l in range(layer_count):
        tables[l][2 * tiles + others] = jnp.zeros((rows, lanes), jnp.bfloat16)

    def turned(x):
        return pltpu.roll(x.astype(jnp.float32), lanes // 2, 1).astype(jnp.bfloat16)

    def exchange(u, l):
        return pltpu.make_async_remote_copy(
            src_ref=going.at[u, l], dst_ref=coming.at[u, l],
            send_sem=going_sem.at[u, l], recv_sem=coming_sem.at[u, l],
            device_id=(my_section, lax.rem(me + 1, part_count)), device_id_type=MESH,
        )

    def send(u, l):
        def one(step, carry):
            peer = lax.rem(me + step, part_count)
            block = wanted_ref[l, peer]
            going[u, l, step - 1] = jnp.where(low, tables[l][block], tables[l][block ^ 1])
            pltpu.make_async_remote_copy(
                src_ref=going.at[u, l, step - 1], dst_ref=coming.at[u, l, step - 1],
                send_sem=going_sem.at[u, l], recv_sem=coming_sem.at[u, l],
                device_id=(my_section, peer), device_id_type=MESH,
            ).start()
            return carry

        lax.fori_loop(1, part_count, one, 0, unroll=min(7, others))

    def enter(u):
        def tile(q, carry):
            x = inbox[u, q]
            tables[0][2 * q] = x
            tables[0][2 * q + 1] = turned(x)
            return carry

        @pl.when((my_section != 0) | (u >= halves))
        def _():
            for c in range(CHUNKS):
                forward(u, c).wait_recv()

        lax.fori_loop(0, tiles, tile, 0, unroll=8)
        send(u, 0)

    def layer(u, l):
        exchange(u, l).wait()

        def arrive(k, carry):
            tables[l][2 * tiles + k] = coming[u, l, k]
            return carry

        lax.fori_loop(0, others, arrive, 0, unroll=min(7, others))

        def quad(g, carry):
            parts = []
            for c in range(4):
                at = (4 * g + c) * 4
                pair = [
                    jnp.where(
                        low,
                        tables[l][source_ref[l, at + 2 * h]],
                        tables[l][source_ref[l, at + 2 * h + 1]],
                    )
                    for h in range(2)
                ]
                parts.append(jnp.concatenate(pair, axis=1))
            left = jnp.concatenate(parts, axis=0)
            summed = lax.dot_general(
                left, flipped[l, g], (((1,), (0,)), ((), ())), preferred_element_type=jnp.float32
            )
            for t in range(2):
                top = 2 * t * rows
                cols = slice(t * lanes, (t + 1) * lanes)
                pre_act = jnp.where(
                    low, summed[top : top + rows, cols], summed[top + rows : top + 2 * rows, cols]
                )
                pre_act = pre_act + bias_ref[l, 2 * g + t]
                result = jnp.clip(pre_act, 0.0, 32.0)
                if l == layer_count - 1:
                    outbox[u, 2 * g + t] = result.astype(jnp.bfloat16)
                else:
                    tables[l + 1][2 * (2 * g + t)] = result.astype(jnp.bfloat16)
                    tables[l + 1][2 * (2 * g + t) + 1] = pltpu.roll(result, lanes // 2, 1).astype(jnp.bfloat16)
            return carry

        if l < layer_count - 1:
            lax.fori_loop(0, quads, quad, 0, unroll=min(8, quads))
            send(u, l + 1)
        else:
            for c in range(CHUNKS):
                lax.fori_loop(c * share, (c + 1) * share, quad, 0, unroll=min(8, share))

                @pl.when(my_section != last)
                def _(c=c):
                    forward(u, c).start()

                @pl.when((my_section == last) & (u < last * halves))
                def _(c=c):
                    deliver(u, c).start()

    @pl.when(my_section == 0)
    def _():
        enter(0)

    for l, load in enumerate(loads):
        load.wait()

        def flip(g, carry, l=l):
            flipped[l, g] = held[l, g].T
            return carry

        lax.fori_loop(0, quads, flip, 0, unroll=min(4, quads))

    @pl.when(my_section != 0)
    def _():
        enter(0)

    def stage(u, carry):
        for l in range(layer_count):
            layer(u, l)
            if l == 0:

                @pl.when(u + 1 < piece_count)
                def _():
                    enter(u + 1)

        return carry

    lax.fori_loop(0, piece_count, stage, 0)

    @pl.when(my_section == last)
    def _():
        own = pltpu.make_async_copy(outbox.at[pl.ds(last * halves, halves)], out_ref, own_sem)
        own.start()
        own.wait()

    @pl.when(my_section != last)
    def _():
        for h, c in pieces:
            deliver(h, c).wait_recv()

    def drain(u, carry):
        @pl.when((my_section != last) | (u < last * halves))
        def _():
            for c in range(CHUNKS):
                forward(u, c).wait_send()

        return carry

    lax.fori_loop(0, piece_count, drain, 0)


def shards(images, weights, bias, pattern, counts):
    section_count = lax.axis_size("section")
    part_count = lax.axis_size("dom")
    my_part = lax.axis_index("dom")
    _, rows, width = images.shape
    layer_count, per_part, block_size, depth = weights.shape
    lanes = 2 * block_size
    halves = rows // PIECE_ROWS
    tiles = width // lanes
    quads = per_part // 4
    others = part_count - 1
    piece_count = section_count * halves
    wanted, source = prepare_tables(pattern, counts, per_part, part_count, my_part)
    tiled_images = images.reshape(halves, PIECE_ROWS, tiles, lanes).transpose(0, 2, 1, 3)
    tiled_weights = weights.reshape(layer_count, quads, 4 * block_size, depth)
    tiled_bias = bias.astype(jnp.float32).reshape(layer_count, tiles, 1, lanes)
    in_vmem = pl.BlockSpec(memory_space=pltpu.VMEM)
    in_smem = pl.BlockSpec(memory_space=pltpu.SMEM)
    dma = pltpu.SemaphoreType.DMA
    flops = 2 * section_count * layer_count * rows * per_part * block_size * depth
    result = pl.pallas_call(
        functools.partial(kernel, section_count, part_count, halves),
        out_shape=jax.ShapeDtypeStruct((halves, tiles, PIECE_ROWS, lanes), jnp.bfloat16),
        in_specs=[in_smem, in_smem, in_vmem, pl.BlockSpec(memory_space=pl.ANY), in_vmem],
        out_specs=in_vmem,
        scratch_shapes=[
            pltpu.VMEM(tiled_weights.shape, jnp.bfloat16),
            pltpu.VMEM((layer_count, quads, depth, 4 * block_size), jnp.bfloat16),
            pltpu.VMEM((piece_count, tiles, PIECE_ROWS, lanes), jnp.bfloat16),
            pltpu.VMEM((piece_count, tiles, PIECE_ROWS, lanes), jnp.bfloat16),
            pltpu.VMEM((piece_count, layer_count, others, PIECE_ROWS, lanes), jnp.bfloat16),
            pltpu.VMEM((piece_count, layer_count, others, PIECE_ROWS, lanes), jnp.bfloat16),
            dma((layer_count,)),
            dma,
            dma((halves, CHUNKS)),
            dma((piece_count, CHUNKS)),
            dma((piece_count, CHUNKS)),
            dma((halves, CHUNKS)),
            dma((piece_count, layer_count)),
            dma((piece_count, layer_count)),
            pltpu.SemaphoreType.REGULAR,
        ]
        + [pltpu.VMEM((2 * tiles + part_count, PIECE_ROWS, lanes), jnp.bfloat16)] * layer_count,
        compiler_params=pltpu.CompilerParams(
            collective_id=0, has_side_effects=True, vmem_limit_bytes=58 * 2**20
        ),
        cost_estimate=pl.CostEstimate(flops=flops, bytes_accessed=2 * weights.size, transcendentals=0),
    )(wanted, source, tiled_images, tiled_weights, tiled_bias)
    return result.transpose(0, 2, 1, 3).reshape(1, rows, width)


def solution(mesh):
    placed = (
        P("section", None, "dom"),
        P("section", "dom", None, None),
        P("section", "dom"),
        P("section", None, None),
        P("section", "dom"),
    )
    return jax.shard_map(
        shards, mesh=mesh, in_specs=placed, out_specs=P("section", None, "dom"), check_vma=False
    )
```
